768 devices in a mesh: intra: 64 (over x, y, z_hi), inter: 12 (over z_lo, core).
Axes of the slice: x: 4, y: 8, z: 12 (z_hi: 2, z_lo: 6; z = z_hi * 6 + z_lo), core: 2. Of those that a mesh axis runs over, the one named last changes fastest.
Arguments:
- tokens: bfloat16 [320, 8192], P(None, 'intra'), may hold values from -6 to 6
- grad_out: bfloat16 [320, 8192], P(None, 'intra'), may hold values from -1 to 1
- up_codes: int32 [8192, 30720], P('intra', 'inter'), may hold values from -127 to 127
- up_scales: float32 [8192, 120], P('intra', 'inter'), may hold values from 6.629126e-05 to 0.0003314563
- down_codes: int32 [8192, 30720], P('intra', 'inter'), may hold values from -127 to 127
- down_scales: float32 [8192, 120], P('intra', 'inter'), may hold values from 6.629126e-05 to 0.0003314563
Outputs:
- grad_up: bfloat16 [8192, 30720], P('intra', 'inter')
- grad_down: bfloat16 [8192, 30720], P('intra', 'inter')
- grad_tokens: bfloat16 [320, 8192], P(None, 'intra')
The draws below stay inside these ranges and needn't reach their ends.
All inputs are finite; a program needn't handle non-finite values.
Results may differ from the reference program's by a relative error of at most 0.007.
Values may be sent and summed in bfloat16 or wider, within the bound.
No kernel may reach another device: no remote copies, remote signals or barrier semaphores. Data moves between devices by JAX's collectives and lax.ppermute only.
A program may use at most 64 MiB of HBM per device.

```python
import math
import jax
import jax.numpy as jnp
from jax import lax

D = 8192
FF_DEV = 2560
TOK = 320
FF = 30720


def plant(array, stream_key, low, high):
    dims = array.shape
    spot = [jax.random.randint(jax.random.fold_in(stream_key, axis), (), 0, dims[axis]) for axis in range(len(dims))]
    array = array.at[tuple(spot)].set(low)
    longest = dims.index(max(dims))
    spot[longest] = (spot[longest] + 1) % dims[longest]
    return array.at[tuple(spot)].set(high)


def levels(own_key, dims, cuts, smallest, largest):
    loudness = 1.0
    for position, shards_of in cuts:
        heights = jax.random.uniform(jax.random.fold_in(jax.random.fold_in(own_key, 6), position), (shards_of,), jnp.float32, smallest / len(cuts), largest / len(cuts))
        loudness = loudness * jnp.repeat(jnp.exp(heights), dims[position] // shards_of).reshape((-1,) + (1,) * (len(dims) - 1 - position))
    return loudness


def bell_draw(key, shape, deviation, bound, shards=(), kind=jnp.bfloat16):
    factor_of = levels(key, shape, shards, -0.22, 0.18) if shards else 1.0
    result = jax.random.normal(key, shape, jnp.float32) * deviation * factor_of
    return jnp.minimum(jnp.maximum(result, -bound), bound).astype(kind)


def setup_inputs(seed: int = 0) -> dict:
    splits = jax.random.split(jax.random.key(seed), 7)
    return {
        "tokens": bell_draw(splits[0], (TOK, D), 1.0, 6.0, ((1, 64),)),
        "grad_out": bell_draw(splits[1], (TOK, D), (3.0 / TOK ** 0.5), 1.0, ((1, 64),)),
        "up_codes": plant(jax.random.randint(splits[2], (D, FF), -127, 128), jax.random.fold_in(splits[2], 1), -127, 127).astype(jnp.int32),
        "up_scales": jnp.clip(jnp.exp(math.log(0.0003314563) - 1.609438 * jax.random.uniform(splits[3], (D, FF // 256), jnp.float32) ** levels(splits[3], (D, FF // 256), ((0, 64), (1, 12)), -0.2, 0.2)), 6.629125709878281e-05, 0.0003314563),
        "down_codes": plant(jax.random.randint(splits[4], (D, FF), -127, 128), jax.random.fold_in(splits[4], 1), -127, 127).astype(jnp.int32),
        "down_scales": jnp.clip(jnp.exp(math.log(0.0003314563) - 1.609438 * jax.random.uniform(splits[5], (D, FF // 256), jnp.float32) ** levels(splits[5], (D, FF // 256), ((0, 64), (1, 12)), -0.2, 0.2)), 6.629125709878281e-05, 0.0003314563),
    }


coef = math.sqrt(2.0 / math.pi)

def gelu_parts(pre):
    inner = coef * (pre + 0.044715 * pre * pre * pre)
    tanh_value = jnp.tanh(inner)
    value = 0.5 * pre * (1.0 + tanh_value)
    slope = 0.5 * (1.0 + tanh_value) + 0.5 * pre * (1.0 - tanh_value * tanh_value) * coef * (1.0 + 3.0 * 0.044715 * pre * pre)
    return (value, slope)

def dequantize(codes, scales):
    rows = codes.shape[0]
    units = codes.shape[1]
    shaped = codes.astype(jnp.float32).reshape(rows, units // 256, 256)
    return (shaped * scales[:, :, None]).reshape(rows, units).astype(jnp.bfloat16)

def reference(tokens, grad_out, up_codes, up_scales, down_codes, down_scales):
    features = tokens.shape[1]
    units = up_codes.shape[1]
    blocks = units // FF_DEV
    contract = (((0,), (0,)), ((), ()))
    across = (((1,), (1,)), ((), ()))

    def step(index, carry):
        grad_up, grad_down, input_sum = carry
        start = (index * FF_DEV).astype(jnp.int32)
        scale_start = (index * (FF_DEV // 256)).astype(jnp.int32)
        w_up = dequantize(lax.dynamic_slice_in_dim(up_codes, start, FF_DEV, 1), lax.dynamic_slice_in_dim(up_scales, scale_start, FF_DEV // 256, 1))
        w_down = dequantize(lax.dynamic_slice_in_dim(down_codes, start, FF_DEV, 1), lax.dynamic_slice_in_dim(down_scales, scale_start, FF_DEV // 256, 1))
        pre = jnp.dot(tokens, w_up, preferred_element_type=jnp.float32)
        back = jnp.dot(grad_out, w_down, preferred_element_type=jnp.float32)
        value, slope = gelu_parts(pre)
        hidden = value.astype(jnp.bfloat16)
        dpre = (back * slope).astype(jnp.bfloat16)
        up_block = lax.dot_general(tokens, dpre, contract, preferred_element_type=jnp.float32).astype(grad_up.dtype)
        down_block = lax.dot_general(grad_out, hidden, contract, preferred_element_type=jnp.float32).astype(grad_down.dtype)
        grad_up = lax.dynamic_update_slice_in_dim(grad_up, up_block, start, 1)
        grad_down = lax.dynamic_update_slice_in_dim(grad_down, down_block, start, 1)
        input_sum = input_sum + lax.dot_general(dpre, w_up, across, preferred_element_type=jnp.float32)
        return (grad_up, grad_down, input_sum)
    init = (jnp.zeros((features, units), jnp.bfloat16), jnp.zeros((features, units), jnp.bfloat16), jnp.zeros((tokens.shape[0], features), jnp.float32))
    grad_up, grad_down, input_sum = lax.fori_loop(0, blocks, step, init)
    return (grad_up, grad_down, input_sum.astype(jnp.bfloat16))
```

```python
import functools
import math

import jax
import jax.numpy as jnp
from jax import lax
from jax.experimental import pallas as pl
from jax.experimental.pallas import tpu as pltpu
from jax.sharding import Mesh
from jax.sharding import PartitionSpec as P

coef = math.sqrt(2.0 / math.pi)
f32 = jnp.float32
bf16 = jnp.bfloat16
LANES = 128
SCALE_BLOCK = 256


def gelu_parts(pre):
    inner = coef * (pre + 0.044715 * pre * pre * pre)
    tanh_value = jnp.tanh(inner)
    value = 0.5 * pre * (1.0 + tanh_value)
    slope = 0.5 * (1.0 + tanh_value) + 0.5 * pre * (1.0 - tanh_value * tanh_value) * coef * (
        1.0 + 3.0 * 0.044715 * pre * pre
    )
    return (value, slope)


def call(kernel, out_shape, *args, name):
    vmem = pl.BlockSpec(memory_space=pltpu.VMEM)
    return pl.pallas_call(
        kernel,
        out_shape=out_shape,
        in_specs=[vmem] * len(args),
        out_specs=jax.tree.map(lambda _: vmem, out_shape),
        compiler_params=pltpu.CompilerParams(vmem_limit_bytes=48 * 1024 * 1024),
        name=name,
    )(*args)


def pack_kernel(nx, tok_ref, grad_ref, uc_ref, us_ref, dc_ref, ds_ref, out_ref):
    feats, units = uc_ref.shape
    tok = tok_ref.shape[0]
    blocks = units // nx // LANES
    for s, (codes, scales, acts) in enumerate(((uc_ref, us_ref, tok_ref), (dc_ref, ds_ref, grad_ref))):
        for x in range(nx):
            for k in range(blocks):
                at = (x * blocks + k) * LANES
                b = at // SCALE_BLOCK
                w = codes[:, at : at + LANES].astype(f32) * scales[:, b : b + 1]
                out_ref[2 * x + s, k * feats : (k + 1) * feats, :] = w.astype(bf16)
            out_ref[2 * x + s, blocks * feats :, :] = acts[...]


def forward_kernel(feats, got_ref, out_ref):
    srcs = got_ref.shape[0]
    blocks = out_ref.shape[1] // LANES
    for k in range(blocks):
        total = None
        for s in range(srcs):
            part = jnp.dot(
                got_ref[s, blocks * feats :, :],
                got_ref[s, k * feats : (k + 1) * feats, :],
                preferred_element_type=f32,
            )
            total = part if total is None else total + part
        out_ref[:, k * LANES : (k + 1) * LANES] = total.astype(bf16)


def sum_kernel(got_ref, keep_ref, send_ref):
    for s in range(2):
        total = got_ref[s].astype(f32)
        for h in range(1, got_ref.shape[0] // 2):
            total = total + got_ref[2 * h + s].astype(f32)
        keep_ref[s] = total
        send_ref[s] = total.astype(bf16)


def gelu_kernel(keep_ref, got_ref, out_ref):
    pre = keep_ref[0] + got_ref[0].astype(f32)
    back = keep_ref[1] + got_ref[1].astype(f32)
    value, slope = gelu_parts(pre)
    hidden = value.astype(bf16)
    dpre = (back * slope).astype(bf16)
    for h in range(out_ref.shape[0] // 2):
        out_ref[2 * h] = dpre
        out_ref[2 * h + 1] = hidden


def backward_kernel(feats, got_ref, act_ref, out_ref):
    srcs = got_ref.shape[0]
    blocks = act_ref.shape[1] // LANES
    act = act_ref[...]
    for s in range(srcs):
        acts = got_ref[s, blocks * feats :, :]
        grad = lax.dot_general(acts, act, (((0,), (0,)), ((), ())), preferred_element_type=f32)
        total = None
        for k in range(blocks):
            cols = slice(k * LANES, (k + 1) * LANES)
            out_ref[s, k * feats : (k + 1) * feats, :] = grad[:, cols].astype(bf16)
            part = lax.dot_general(
                act[:, cols],
                got_ref[s, k * feats : (k + 1) * feats, :],
                (((1,), (1,)), ((), ())),
                preferred_element_type=f32,
            )
            total = part if total is None else total + part
        out_ref[s, blocks * feats :, :] = total.astype(bf16)


def input_kernel(at, got_ref, out_ref):
    rows = got_ref.shape[1] - at
    total = got_ref[0, at:, :].astype(f32)
    for x in range(1, got_ref.shape[0] // 2):
        total = total + got_ref[2 * x, at:, :].astype(f32)
    out_ref[:rows, :] = total.astype(bf16)
    if out_ref.shape[0] > rows:
        out_ref[rows:, :] = jnp.zeros((out_ref.shape[0] - rows, LANES), bf16)


def unpack_kernel(feats, got_ref, up_ref, down_ref):
    nx = got_ref.shape[0] // 2
    blocks = up_ref.shape[1] // nx // LANES
    for s, out in enumerate((up_ref, down_ref)):
        for x in range(nx):
            for k in range(blocks):
                at = (x * blocks + k) * LANES
                out[:, at : at + LANES] = got_ref[2 * x + s, k * feats : (k + 1) * feats, :]


def reduce_kernel(got_ref, out_ref):
    total = got_ref[0].astype(f32)
    for i in range(1, got_ref.shape[0]):
        total = total + got_ref[i].astype(f32)
    final = total.astype(bf16)
    for i in range(out_ref.shape[0]):
        out_ref[i] = final


def exchange(value, axes):
    return lax.all_to_all(value, axes, 0, 0, tiled=True)


def shards(sizes, tokens, grad_out, up_codes, up_scales, down_codes, down_scales):
    nx, nyh, nyl, nzl, ncore = (sizes[a] for a in ("x", "yh", "yl", "zl", "core"))
    feats, units = up_codes.shape
    tok = tokens.shape[0]
    mine = units // nx
    srcs = nx * nyl
    share = tok // (nyh * nyl)
    rows = feats * (mine // LANES)
    S = jax.ShapeDtypeStruct

    packed = call(
        functools.partial(pack_kernel, nx),
        S((srcs, rows + tok, LANES), bf16),
        tokens, grad_out, up_codes, up_scales, down_codes, down_scales,
        name="pack",
    )
    got = exchange(packed, ("x", "yl"))
    part = call(functools.partial(forward_kernel, feats), S((tok, mine), bf16), got, name="forward")
    terms = exchange(part.reshape(nyh * nyl, share, mine), ("yh", "yl"))
    keep, send = call(
        sum_kernel, (S((2, share, mine), f32), S((2, share, mine), bf16)), terms, name="sum"
    )
    other = lax.ppermute(send, "zh", [(0, 1), (1, 0)])
    acts = call(gelu_kernel, S((nyh * nyl, share, mine), bf16), keep, other, name="gelu")
    act = exchange(acts, ("yh", "yl")).reshape(tok, mine)
    grads = call(
        functools.partial(backward_kernel, feats), S((srcs, rows + tok, LANES), bf16), got, act, name="backward"
    )
    home = exchange(grads, ("x", "yl"))
    inter = nzl * ncore
    slab = -(-tok // (16 * inter)) * 16
    padded = call(functools.partial(input_kernel, rows), S((inter * slab, LANES), bf16), home, name="input")
    slabs = exchange(padded.reshape(inter, slab, LANES), ("zl", "core"))
    final = call(reduce_kernel, S((inter, slab, LANES), bf16), slabs, name="reduce")
    grad_tokens = exchange(final, ("zl", "core")).reshape(inter * slab, LANES)[:tok]
    grad_up, grad_down = call(
        functools.partial(unpack_kernel, feats),
        (S((feats, units), bf16), S((feats, units), bf16)),
        home,
        name="unpack",
    )
    return grad_up, grad_down, grad_tokens


AXES = ("x", "yh", "yl", "zh", "zl", "core")
SIZES = (4, 4, 2, 2, 6, 2)


def solution(mesh, sizes=SIZES):
    fine = Mesh(mesh.devices.reshape(sizes), AXES)
    intra, inter = AXES[:4], AXES[4:]
    in_specs = (
        P(None, intra),
        P(None, intra),
        P(intra, inter),
        P(intra, inter),
        P(intra, inter),
        P(intra, inter),
    )
    out_specs = (P(intra, inter), P(intra, inter), P(None, intra))
    return jax.shard_map(
        functools.partial(shards, dict(zip(AXES, sizes))),
        mesh=fine,
        in_specs=in_specs,
        out_specs=out_specs,
        check_vma=False,
    )
```

```python
import functools
import math

import jax
import jax.numpy as jnp
from jax import lax
from jax.experimental import pallas as pl
from jax.experimental.pallas import tpu as pltpu
from jax.sharding import Mesh
from jax.sharding import PartitionSpec as P

coef = math.sqrt(2.0 / math.pi)
f32 = jnp.float32
bf16 = jnp.bfloat16
LANES = 128
SCALE_BLOCK = 256


def gelu_parts(pre):
    inner = coef * (pre + 0.044715 * pre * pre * pre)
    tanh_value = jnp.tanh(inner)
    value = 0.5 * pre * (1.0 + tanh_value)
    slope = 0.5 * (1.0 + tanh_value) + 0.5 * pre * (1.0 - tanh_value * tanh_value) * coef * (
        1.0 + 3.0 * 0.044715 * pre * pre
    )
    return (value, slope)


def call(kernel, out_shape, *args, name):
    vmem = pl.BlockSpec(memory_space=pltpu.VMEM)
    return pl.pallas_call(
        kernel,
        out_shape=out_shape,
        in_specs=[vmem] * len(args),
        out_specs=jax.tree.map(lambda _: vmem, out_shape),
        compiler_params=pltpu.CompilerParams(vmem_limit_bytes=48 * 1024 * 1024),
        name=name,
    )(*args)


def pack_kernel(nx, tok_ref, grad_ref, uc_ref, us_ref, dc_ref, ds_ref, out_ref, codes, scales, sems, act_sems):
    feats, units = uc_ref.shape
    width = units // nx
    blocks = width // LANES
    sides = ((uc_ref, us_ref, tok_ref), (dc_ref, ds_ref, grad_ref))
    scale_copies = [
        pltpu.make_async_copy(side[1], scales.at[s], sems.at[s, nx]) for s, side in enumerate(sides)
    ]
    for copy in scale_copies:
        copy.start()
    code_copies = {}
    for x in range(nx):
        for s, side in enumerate(sides):
            cols = pl.ds(x * width, width)
            code_copies[s, x] = pltpu.make_async_copy(
                side[0].at[:, cols], codes.at[s, :, cols], sems.at[s, x]
            )
            code_copies[s, x].start()
    act_copies = []
    for x in range(nx):
        for s, side in enumerate(sides):
            act_copies.append(
                pltpu.make_async_copy(
                    side[2],
                    out_ref.at[2 * x + s, pl.ds(blocks * feats, tok_ref.shape[0]), :],
                    act_sems.at[2 * x + s],
                )
            )
            act_copies[-1].start()
    columns = []
    for s in range(2):
        scale_copies[s].wait()
        columns.append(scales[s].T)
    for x in range(nx):
        for s in range(2):
            code_copies[s, x].wait()
            for k in range(blocks):
                at = (x * blocks + k) * LANES
                b = at // SCALE_BLOCK
                w = codes[s, :, at : at + LANES].astype(f32) * columns[s][:, b : b + 1]
                out_ref[2 * x + s, k * feats : (k + 1) * feats, :] = w.astype(bf16)
    for copy in act_copies:
        copy.wait()


def pack(nx, tokens, grad_out, up_codes, up_scales, down_codes, down_scales):
    feats, units = up_codes.shape
    tok = tokens.shape[0]
    rows = feats * (units // nx // LANES)
    return pl.pallas_call(
        functools.partial(pack_kernel, nx),
        out_shape=jax.ShapeDtypeStruct((2 * nx, rows + tok, LANES), bf16),
        in_specs=[pl.BlockSpec(memory_space=pltpu.HBM)] * 6,
        out_specs=pl.BlockSpec(memory_space=pltpu.VMEM),
        scratch_shapes=[
            pltpu.VMEM((2, feats, units), jnp.int32),
            pltpu.VMEM((2, units // SCALE_BLOCK, feats), f32),
            pltpu.SemaphoreType.DMA((2, nx + 1)),
            pltpu.SemaphoreType.DMA((2 * nx,)),
        ],
        compiler_params=pltpu.CompilerParams(vmem_limit_bytes=56 * 1024 * 1024),
        name="pack",
    )(tokens, grad_out, up_codes, up_scales.T, down_codes, down_scales.T)


def forward_kernel(feats, got_ref, out_ref):
    srcs = got_ref.shape[0]
    blocks = out_ref.shape[1] // LANES
    for k in range(blocks):
        total = None
        for s in range(srcs):
            part = jnp.dot(
                got_ref[s, blocks * feats :, :],
                got_ref[s, k * feats : (k + 1) * feats, :],
                preferred_element_type=f32,
            )
            total = part if total is None else total + part
        out_ref[:, k * LANES : (k + 1) * LANES] = total.astype(bf16)


def sum_kernel(got_ref, keep_ref, send_ref):
    for s in range(2):
        total = got_ref[s].astype(f32)
        for h in range(1, got_ref.shape[0] // 2):
            total = total + got_ref[2 * h + s].astype(f32)
        keep_ref[s] = total
        send_ref[s] = total.astype(bf16)


def gelu_kernel(keep_ref, got_ref, out_ref):
    pre = keep_ref[0] + got_ref[0].astype(f32)
    back = keep_ref[1] + got_ref[1].astype(f32)
    value, slope = gelu_parts(pre)
    hidden = value.astype(bf16)
    dpre = (back * slope).astype(bf16)
    for h in range(out_ref.shape[0] // 2):
        out_ref[2 * h] = dpre
        out_ref[2 * h + 1] = hidden


def terms_kernel(feats, got_ref, act_ref, out_ref):
    blocks = act_ref.shape[1] // LANES
    act = act_ref[...]
    for s in range(got_ref.shape[0]):
        total = None
        for k in range(blocks):
            part = lax.dot_general(
                act[:, k * LANES : (k + 1) * LANES],
                got_ref[s, k * feats : (k + 1) * feats, :],
                (((1,), (1,)), ((), ())),
                preferred_element_type=f32,
            )
            total = part if total is None else total + part
        out_ref[s] = total.astype(bf16)


def grads_kernel(feats, got_ref, act_ref, out_ref):
    blocks = act_ref.shape[1] // LANES
    act = act_ref[...]
    for s in range(got_ref.shape[0]):
        acts = got_ref[s, blocks * feats :, :]
        grad = lax.dot_general(acts, act, (((0,), (0,)), ((), ())), preferred_element_type=f32)
        for k in range(blocks):
            out_ref[s, k * feats : (k + 1) * feats, :] = grad[:, k * LANES : (k + 1) * LANES].astype(bf16)


def home_kernel(got_ref, out_ref):
    total = got_ref[0].astype(f32)
    for x in range(1, got_ref.shape[0] // 2):
        total = total + got_ref[2 * x].astype(f32)
    out_ref[...] = total


def pair_kernel(a_ref, b_ref, out_ref):
    out_ref[...] = (a_ref[...] + b_ref[...]).astype(out_ref.dtype)


def triple_kernel(own_ref, prev_ref, next_ref, out_ref):
    pos = lax.div(lax.axis_index("zl"), 2)
    own, prev, nxt = (r[...].astype(f32) for r in (own_ref, prev_ref, next_ref))
    first = jnp.where(pos == 0, own, jnp.where(pos == 1, prev, nxt))
    second = jnp.where(pos == 1, own, jnp.where(pos == 2, prev, nxt))
    third = jnp.where(pos == 2, own, jnp.where(pos == 0, prev, nxt))
    out_ref[...] = (first + second + third).astype(bf16)


def unpack_kernel(feats, got_ref, up_ref, down_ref):
    nx = got_ref.shape[0] // 2
    blocks = up_ref.shape[1] // nx // LANES
    for s, out in enumerate((up_ref, down_ref)):
        for x in range(nx):
            for k in range(blocks):
                at = (x * blocks + k) * LANES
                out[:, at : at + LANES] = got_ref[2 * x + s, k * feats : (k + 1) * feats, :]


def exchange(value, axes):
    return lax.all_to_all(value, axes, 0, 0, tiled=True)


def inter_sum(nzl, ncore, term):
    S = jax.ShapeDtypeStruct
    other = lax.ppermute(term, "core", [(i, i ^ 1) for i in range(ncore)])
    term = call(pair_kernel, S(term.shape, f32), term, other, name="cores")
    other = lax.ppermute(term, "zl", [(i, i ^ 1) for i in range(nzl)])
    term = call(pair_kernel, S(term.shape, bf16), term, other, name="pairs")
    prev = lax.ppermute(term, "zl", [(i, (i + 2) % nzl) for i in range(nzl)])
    nxt = lax.ppermute(term, "zl", [(i, (i - 2) % nzl) for i in range(nzl)])
    return call(triple_kernel, S(term.shape, bf16), term, prev, nxt, name="triples")


def shards(sizes, tokens, grad_out, up_codes, up_scales, down_codes, down_scales):
    nx, nyh, nyl, nzl, ncore = (sizes[a] for a in ("x", "yh", "yl", "zl", "core"))
    feats, units = up_codes.shape
    tok = tokens.shape[0]
    mine = units // nx
    srcs = nx * nyl
    share = tok // (nyh * nyl)
    rows = feats * (mine // LANES)
    S = jax.ShapeDtypeStruct

    packed = pack(nx, tokens, grad_out, up_codes, up_scales, down_codes, down_scales)
    got = exchange(packed, ("x", "yl"))
    part = call(functools.partial(forward_kernel, feats), S((tok, mine), bf16), got, name="forward")
    terms = exchange(part.reshape(nyh * nyl, share, mine), ("yh", "yl"))
    keep, send = call(
        sum_kernel, (S((2, share, mine), f32), S((2, share, mine), bf16)), terms, name="sum"
    )
    other = lax.ppermute(send, "zh", [(0, 1), (1, 0)])
    acts = call(gelu_kernel, S((nyh * nyl, share, mine), bf16), keep, other, name="gelu")
    act = exchange(acts, ("yh", "yl")).reshape(tok, mine)
    terms = call(functools.partial(terms_kernel, feats), S((srcs, tok, feats), bf16), got, act, name="terms")
    terms = exchange(terms, ("x", "yl"))
    grads = call(functools.partial(grads_kernel, feats), S((srcs, rows, LANES), bf16), got, act, name="grads")
    home = exchange(grads, ("x", "yl"))
    grad_tokens = inter_sum(nzl, ncore, call(home_kernel, S((tok, feats), f32), terms, name="home"))
    grad_up, grad_down = call(
        functools.partial(unpack_kernel, feats),
        (S((feats, units), bf16), S((feats, units), bf16)),
        home,
        name="unpack",
    )
    return grad_up, grad_down, grad_tokens


AXES = ("x", "yh", "yl", "zh", "zl", "core")
SIZES = (4, 4, 2, 2, 6, 2)


def solution(mesh, sizes=SIZES):
    fine = Mesh(mesh.devices.reshape(sizes), AXES)
    intra, inter = AXES[:4], AXES[4:]
    in_specs = (
        P(None, intra),
        P(None, intra),
        P(intra, inter),
        P(intra, inter),
        P(intra, inter),
        P(intra, inter),
    )
    out_specs = (P(intra, inter), P(intra, inter), P(None, intra))
    return jax.shard_map(
        functools.partial(shards, dict(zip(AXES, sizes))),
        mesh=fine,
        in_specs=in_specs,
        out_specs=out_specs,
        check_vma=False,
    )
```

```python
import functools
import math

import jax
import jax.numpy as jnp
from jax import lax
from jax.experimental import pallas as pl
from jax.experimental.pallas import tpu as pltpu
from jax.sharding import Mesh
from jax.sharding import PartitionSpec as P

coef = math.sqrt(2.0 / math.pi)
f32 = jnp.float32
bf16 = jnp.bfloat16
LANES = 128
SCALE_BLOCK = 256


def gelu_parts(pre):
    inner = coef * (pre + 0.044715 * pre * pre * pre)
    tanh_value = jnp.tanh(inner)
    value = 0.5 * pre * (1.0 + tanh_value)
    slope = 0.5 * (1.0 + tanh_value) + 0.5 * pre * (1.0 - tanh_value * tanh_value) * coef * (
        1.0 + 3.0 * 0.044715 * pre * pre
    )
    return (value, slope)


def call(kernel, out_shape, *args, name):
    vmem = pl.BlockSpec(memory_space=pltpu.VMEM)
    return pl.pallas_call(
        kernel,
        out_shape=out_shape,
        in_specs=[vmem] * len(args),
        out_specs=jax.tree.map(lambda _: vmem, out_shape),
        compiler_params=pltpu.CompilerParams(vmem_limit_bytes=48 * 1024 * 1024),
        name=name,
    )(*args)


def pack_kernel(nx, tok_ref, grad_ref, uc_ref, us_ref, dc_ref, ds_ref, out_ref, codes, scales, packed, sems, act_sems, out_sems):
    feats, units = uc_ref.shape
    width = units // nx
    blocks = width // LANES
    sides = ((uc_ref, us_ref, tok_ref), (dc_ref, ds_ref, grad_ref))
    scale_copies = [
        pltpu.make_async_copy(side[1], scales.at[s], sems.at[s, nx]) for s, side in enumerate(sides)
    ]
    for copy in scale_copies:
        copy.start()
    code_copies = {}
    for x in range(nx):
        for s, side in enumerate(sides):
            cols = pl.ds(x * width, width)
            code_copies[s, x] = pltpu.make_async_copy(
                side[0].at[:, cols], codes.at[s, :, cols], sems.at[s, x]
            )
            code_copies[s, x].start()
    pending = []
    for x in range(nx):
        for s, side in enumerate(sides):
            pending.append(
                pltpu.make_async_copy(
                    side[2],
                    out_ref.at[2 * x + s, pl.ds(blocks * feats, tok_ref.shape[0]), :],
                    act_sems.at[2 * x + s],
                )
            )
            pending[-1].start()
    columns = []
    for s in range(2):
        scale_copies[s].wait()
        columns.append(scales[s].T)
    for x in range(nx):
        for s in range(2):
            code_copies[s, x].wait()
            for k in range(blocks):
                at = (x * blocks + k) * LANES
                b = at // SCALE_BLOCK
                w = codes[s, :, at : at + LANES].astype(f32) * columns[s][:, b : b + 1]
                packed[2 * x + s, k * feats : (k + 1) * feats, :] = w.astype(bf16)
            pending.append(
                pltpu.make_async_copy(
                    packed.at[2 * x + s],
                    out_ref.at[2 * x + s, pl.ds(0, blocks * feats), :],
                    out_sems.at[2 * x + s],
                )
            )
            pending[-1].start()
    for copy in pending:
        copy.wait()


def pack(nx, tokens, grad_out, up_codes, up_scales, down_codes, down_scales):
    feats, units = up_codes.shape
    tok = tokens.shape[0]
    rows = feats * (units // nx // LANES)
    return pl.pallas_call(
        functools.partial(pack_kernel, nx),
        out_shape=jax.ShapeDtypeStruct((2 * nx, rows + tok, LANES), bf16),
        in_specs=[pl.BlockSpec(memory_space=pltpu.HBM)] * 6,
        out_specs=pl.BlockSpec(memory_space=pltpu.HBM),
        scratch_shapes=[
            pltpu.VMEM((2, feats, units), jnp.int32),
            pltpu.VMEM((2, units // SCALE_BLOCK, feats), f32),
            pltpu.VMEM((2 * nx, rows, LANES), bf16),
            pltpu.SemaphoreType.DMA((2, nx + 1)),
            pltpu.SemaphoreType.DMA((2 * nx,)),
            pltpu.SemaphoreType.DMA((2 * nx,)),
        ],
        compiler_params=pltpu.CompilerParams(vmem_limit_bytes=56 * 1024 * 1024),
        name="pack",
    )(tokens, grad_out, up_codes, up_scales.T, down_codes, down_scales.T)


def forward_kernel(feats, got_ref, out_ref):
    srcs = got_ref.shape[0]
    blocks = out_ref.shape[1] // LANES
    for k in range(blocks):
        total = None
        for s in range(srcs):
            part = jnp.dot(
                got_ref[s, blocks * feats :, :],
                got_ref[s, k * feats : (k + 1) * feats, :],
                preferred_element_type=f32,
            )
            total = part if total is None else total + part
        out_ref[:, k * LANES : (k + 1) * LANES] = total.astype(bf16)


def sum_kernel(got_ref, keep_ref, send_ref):
    for s in range(2):
        total = got_ref[s].astype(f32)
        for h in range(1, got_ref.shape[0] // 2):
            total = total + got_ref[2 * h + s].astype(f32)
        keep_ref[s] = total
        send_ref[s] = total.astype(bf16)


def gelu_kernel(keep_ref, got_ref, out_ref):
    pre = keep_ref[0] + got_ref[0].astype(f32)
    back = keep_ref[1] + got_ref[1].astype(f32)
    value, slope = gelu_parts(pre)
    hidden = value.astype(bf16)
    dpre = (back * slope).astype(bf16)
    for h in range(out_ref.shape[0] // 2):
        out_ref[2 * h] = dpre
        out_ref[2 * h + 1] = hidden


def terms_kernel(feats, theirs, got_ref, act_ref, out_ref):
    blocks = act_ref.shape[1] // LANES
    half = act_ref.shape[0] // 2
    core = lax.axis_index("core")
    start = pl.multiple_of((1 - core if theirs else core) * half, half)
    act = act_ref[pl.ds(start, half), :]
    for s in range(got_ref.shape[0]):
        total = None
        for k in range(blocks):
            part = lax.dot_general(
                act[:, k * LANES : (k + 1) * LANES],
                got_ref[s, k * feats : (k + 1) * feats, :],
                (((1,), (1,)), ((), ())),
                preferred_element_type=f32,
            )
            total = part if total is None else total + part
        out_ref[s] = total.astype(out_ref.dtype)


def grads_kernel(feats, got_ref, act_ref, out_ref):
    blocks = act_ref.shape[1] // LANES
    act = act_ref[...]
    for s in range(got_ref.shape[0]):
        acts = got_ref[s, blocks * feats :, :]
        grad = lax.dot_general(acts, act, (((0,), (0,)), ((), ())), preferred_element_type=f32)
        for k in range(blocks):
            out_ref[s, k * feats : (k + 1) * feats, :] = grad[:, k * LANES : (k + 1) * LANES].astype(bf16)


def pair_kernel(keep_ref, got_ref, out_ref):
    out_ref[...] = (keep_ref[...] + got_ref[...].astype(f32)).astype(bf16)


def home_kernel(got_ref, out_ref):
    total = got_ref[0].astype(f32)
    for x in range(1, got_ref.shape[0] // 2):
        total = total + got_ref[2 * x].astype(f32)
    out_ref[...] = total


def triple_kernel(own_ref, prev_ref, next_ref, out_ref):
    pos = lax.div(lax.axis_index("zl"), 2)
    own, prev, nxt = (r[...].astype(f32) for r in (own_ref, prev_ref, next_ref))
    first = jnp.where(pos == 0, own, jnp.where(pos == 1, prev, nxt))
    second = jnp.where(pos == 1, own, jnp.where(pos == 2, prev, nxt))
    third = jnp.where(pos == 2, own, jnp.where(pos == 0, prev, nxt))
    out_ref[...] = (first + second + third).astype(bf16)


def halves_kernel(own_ref, other_ref, out_ref):
    half = own_ref.shape[0]
    core = lax.axis_index("core")
    out_ref[pl.ds(pl.multiple_of(core * half, half), half), :] = own_ref[...]
    out_ref[pl.ds(pl.multiple_of((1 - core) * half, half), half), :] = other_ref[...]


def unpack_kernel(feats, got_ref, up_ref, down_ref, sems):
    nx = got_ref.shape[0] // 2
    blocks = up_ref.shape[1] // nx // LANES
    copies = []
    for x in range(nx):
        for s, out in enumerate((up_ref, down_ref)):
            for k in range(blocks):
                copies.append(
                    pltpu.make_async_copy(
                        got_ref.at[2 * x + s, pl.ds(k * feats, feats), :],
                        out.at[:, pl.ds((x * blocks + k) * LANES, LANES)],
                        sems.at[len(copies)],
                    )
                )
                copies[-1].start()
    for copy in copies:
        copy.wait()


def unpack(feats, units, got):
    out = jax.ShapeDtypeStruct((feats, units), bf16)
    hbm = pl.BlockSpec(memory_space=pltpu.HBM)
    return pl.pallas_call(
        functools.partial(unpack_kernel, feats),
        out_shape=(out, out),
        in_specs=[pl.BlockSpec(memory_space=pltpu.VMEM)],
        out_specs=(hbm, hbm),
        scratch_shapes=[pltpu.SemaphoreType.DMA((2 * units // LANES,))],
        compiler_params=pltpu.CompilerParams(vmem_limit_bytes=48 * 1024 * 1024),
        name="unpack",
    )(got)


def exchange(value, axes):
    return lax.all_to_all(value, axes, 0, 0, tiled=True)


def shards(sizes, tokens, grad_out, up_codes, up_scales, down_codes, down_scales):
    nx, nyh, nyl, nzl, ncore = (sizes[a] for a in ("x", "yh", "yl", "zl", "core"))
    feats, units = up_codes.shape
    tok = tokens.shape[0]
    mine = units // nx
    srcs = nx * nyl
    share = tok // (nyh * nyl)
    rows = feats * (mine // LANES)
    S = jax.ShapeDtypeStruct

    packed = pack(nx, tokens, grad_out, up_codes, up_scales, down_codes, down_scales)
    got = exchange(packed, ("x", "yl"))
    part = call(functools.partial(forward_kernel, feats), S((tok, mine), bf16), got, name="forward")
    terms = exchange(part.reshape(nyh * nyl, share, mine), ("yh", "yl"))
    keep, send = call(
        sum_kernel, (S((2, share, mine), f32), S((2, share, mine), bf16)), terms, name="sum"
    )
    other = lax.ppermute(send, "zh", [(0, 1), (1, 0)])
    acts = call(gelu_kernel, S((nyh * nyl, share, mine), bf16), keep, other, name="gelu")
    act = exchange(acts, ("yh", "yl")).reshape(tok, mine)
    half = tok // 2
    swap = [(i, i ^ 1) for i in range(ncore)]
    send = call(
        functools.partial(terms_kernel, feats, True), S((srcs, half, feats), bf16), got, act, name="terms_send"
    )
    other = lax.ppermute(send, "core", swap)
    grads = call(functools.partial(grads_kernel, feats), S((srcs, rows, LANES), bf16), got, act, name="grads")
    keep = call(
        functools.partial(terms_kernel, feats, False), S((srcs, half, feats), f32), got, act, name="terms_keep"
    )
    terms = exchange(call(pair_kernel, S((srcs, half, feats), bf16), keep, other, name="pair"), ("x", "yl"))
    home = exchange(grads, ("x", "yl"))
    term = call(home_kernel, S((half, feats), f32), terms, name="home")
    other = lax.ppermute(term, "zl", [(i, i ^ 1) for i in range(nzl)])
    term = call(pair_kernel, S((half, feats), bf16), term, other, name="pairs")
    prev = lax.ppermute(term, "zl", [(i, (i + 2) % nzl) for i in range(nzl)])
    nxt = lax.ppermute(term, "zl", [(i, (i - 2) % nzl) for i in range(nzl)])
    final = call(triple_kernel, S((half, feats), bf16), term, prev, nxt, name="triples")
    grad_tokens = call(
        halves_kernel, S((tok, feats), bf16), final, lax.ppermute(final, "core", swap), name="halves"
    )
    grad_up, grad_down = unpack(feats, units, home)
    return grad_up, grad_down, grad_tokens


AXES = ("x", "yh", "yl", "zh", "zl", "core")
SIZES = (4, 4, 2, 2, 6, 2)


def solution(mesh, sizes=SIZES):
    fine = Mesh(mesh.devices.reshape(sizes), AXES)
    intra, inter = AXES[:4], AXES[4:]
    in_specs = (
        P(None, intra),
        P(None, intra),
        P(intra, inter),
        P(intra, inter),
        P(intra, inter),
        P(intra, inter),
    )
    out_specs = (P(intra, inter), P(intra, inter), P(None, intra))
    return jax.shard_map(
        functools.partial(shards, dict(zip(AXES, sizes))),
        mesh=fine,
        in_specs=in_specs,
        out_specs=out_specs,
        check_vma=False,
    )
```

```python
import functools
import math

import jax
import jax.numpy as jnp
from jax import lax
from jax.experimental import pallas as pl
from jax.experimental.pallas import tpu as pltpu
from jax.sharding import Mesh
from jax.sharding import PartitionSpec as P

coef = math.sqrt(2.0 / math.pi)
f32 = jnp.float32
bf16 = jnp.bfloat16
LANES = 128
SCALE_BLOCK = 256


def gelu_parts(pre):
    inner = coef * (pre + 0.044715 * pre * pre * pre)
    tanh_value = jnp.tanh(inner)
    value = 0.5 * pre * (1.0 + tanh_value)
    slope = 0.5 * (1.0 + tanh_value) + 0.5 * pre * (1.0 - tanh_value * tanh_value) * coef * (
        1.0 + 3.0 * 0.044715 * pre * pre
    )
    return (value, slope)


def call(kernel, out_shape, *args, name):
    vmem = pl.BlockSpec(memory_space=pltpu.VMEM)
    return pl.pallas_call(
        kernel,
        out_shape=out_shape,
        in_specs=[vmem] * len(args),
        out_specs=jax.tree.map(lambda _: vmem, out_shape),
        compiler_params=pltpu.CompilerParams(vmem_limit_bytes=48 * 1024 * 1024),
        name=name,
    )(*args)


def pack_kernel(nx, tok_ref, grad_ref, uc_ref, us_ref, dc_ref, ds_ref, out_ref, codes, scales, acts, packed, sems, act_sems, out_sems):
    feats, units = uc_ref.shape
    width = units // nx
    blocks = width // LANES
    sides = ((uc_ref, us_ref, tok_ref), (dc_ref, ds_ref, grad_ref))
    scale_copies = [
        pltpu.make_async_copy(side[1], scales.at[s], sems.at[s, nx]) for s, side in enumerate(sides)
    ]
    for copy in scale_copies:
        copy.start()
    code_copies = {}
    for x in range(nx):
        for s, side in enumerate(sides):
            cols = pl.ds(x * width, width)
            code_copies[s, x] = pltpu.make_async_copy(
                side[0].at[:, cols], codes.at[s, :, cols], sems.at[s, x]
            )
            code_copies[s, x].start()
    act_copies = [pltpu.make_async_copy(side[2], acts.at[s], act_sems.at[s]) for s, side in enumerate(sides)]
    for copy in act_copies:
        copy.start()
    pending = []
    columns = []
    for s in range(2):
        scale_copies[s].wait()
        columns.append(scales[s].T)
    for s in range(2):
        act_copies[s].wait()
        for x in range(nx):
            packed[2 * x + s, blocks * feats :, :] = acts[s]
    for x in range(nx):
        for s in range(2):
            code_copies[s, x].wait()
            for k in range(blocks):
                at = (x * blocks + k) * LANES
                b = at // SCALE_BLOCK
                w = codes[s, :, at : at + LANES].astype(f32) * columns[s][:, b : b + 1]
                packed[2 * x + s, k * feats : (k + 1) * feats, :] = w.astype(bf16)
            pending.append(
                pltpu.make_async_copy(
                    packed.at[2 * x + s], out_ref.at[2 * x + s], out_sems.at[2 * x + s]
                )
            )
            pending[-1].start()
    for copy in pending:
        copy.wait()


def pack(nx, tokens, grad_out, up_codes, up_scales, down_codes, down_scales):
    feats, units = up_codes.shape
    tok = tokens.shape[0]
    rows = feats * (units // nx // LANES)
    return pl.pallas_call(
        functools.partial(pack_kernel, nx),
        out_shape=jax.ShapeDtypeStruct((2 * nx, rows + tok, LANES), bf16),
        in_specs=[pl.BlockSpec(memory_space=pltpu.HBM)] * 6,
        out_specs=pl.BlockSpec(memory_space=pltpu.HBM),
        scratch_shapes=[
            pltpu.VMEM((2, feats, units), jnp.int32),
            pltpu.VMEM((2, units // SCALE_BLOCK, feats), f32),
            pltpu.VMEM((2, tok, LANES), bf16),
            pltpu.VMEM((2 * nx, rows + tok, LANES), bf16),
            pltpu.SemaphoreType.DMA((2, nx + 1)),
            pltpu.SemaphoreType.DMA((2,)),
            pltpu.SemaphoreType.DMA((2 * nx,)),
        ],
        compiler_params=pltpu.CompilerParams(vmem_limit_bytes=56 * 1024 * 1024),
        name="pack",
    )(tokens, grad_out, up_codes, up_scales.T, down_codes, down_scales.T)


def forward_kernel(feats, got_ref, out_ref):
    srcs = got_ref.shape[0]
    blocks = out_ref.shape[1] // LANES
    for k in range(blocks):
        total = None
        for s in range(srcs):
            part = jnp.dot(
                got_ref[s, blocks * feats :, :],
                got_ref[s, k * feats : (k + 1) * feats, :],
                preferred_element_type=f32,
            )
            total = part if total is None else total + part
        out_ref[:, k * LANES : (k + 1) * LANES] = total.astype(bf16)


def sum_kernel(got_ref, keep_ref, send_ref):
    for s in range(2):
        total = got_ref[s].astype(f32)
        for h in range(1, got_ref.shape[0] // 2):
            total = total + got_ref[2 * h + s].astype(f32)
        keep_ref[s] = total
        send_ref[s] = total.astype(bf16)


def gelu_kernel(keep_ref, got_ref, out_ref):
    pre = keep_ref[0] + got_ref[0].astype(f32)
    back = keep_ref[1] + got_ref[1].astype(f32)
    value, slope = gelu_parts(pre)
    hidden = value.astype(bf16)
    dpre = (back * slope).astype(bf16)
    for h in range(out_ref.shape[0] // 2):
        out_ref[2 * h] = dpre
        out_ref[2 * h + 1] = hidden


def terms_kernel(feats, theirs, got_ref, act_ref, out_ref):
    blocks = act_ref.shape[1] // LANES
    half = act_ref.shape[0] // 2
    core = lax.axis_index("core")
    start = pl.multiple_of((1 - core if theirs else core) * half, half)
    act = act_ref[pl.ds(start, half), :]
    for s in range(got_ref.shape[0]):
        total = None
        for k in range(blocks):
            part = lax.dot_general(
                act[:, k * LANES : (k + 1) * LANES],
                got_ref[s, k * feats : (k + 1) * feats, :],
                (((1,), (1,)), ((), ())),
                preferred_element_type=f32,
            )
            total = part if total is None else total + part
        out_ref[s] = total.astype(out_ref.dtype)


def grads_kernel(feats, got_ref, act_ref, out_ref):
    blocks = act_ref.shape[1] // LANES
    act = act_ref[...]
    for s in range(got_ref.shape[0]):
        acts = got_ref[s, blocks * feats :, :]
        grad = lax.dot_general(acts, act, (((0,), (0,)), ((), ())), preferred_element_type=f32)
        for k in range(blocks):
            out_ref[s, k * feats : (k + 1) * feats, :] = grad[:, k * LANES : (k + 1) * LANES].astype(bf16)


def pair_kernel(keep_ref, got_ref, out_ref):
    out_ref[...] = (keep_ref[...] + got_ref[...].astype(f32)).astype(bf16)


def home_kernel(got_ref, out_ref):
    total = got_ref[0].astype(f32)
    for x in range(1, got_ref.shape[0] // 2):
        total = total + got_ref[2 * x].astype(f32)
    out_ref[...] = total


def triple_kernel(own_ref, prev_ref, next_ref, out_ref):
    pos = lax.div(lax.axis_index("zl"), 2)
    own, prev, nxt = (r[...].astype(f32) for r in (own_ref, prev_ref, next_ref))
    first = jnp.where(pos == 0, own, jnp.where(pos == 1, prev, nxt))
    second = jnp.where(pos == 1, own, jnp.where(pos == 2, prev, nxt))
    third = jnp.where(pos == 2, own, jnp.where(pos == 0, prev, nxt))
    out_ref[...] = (first + second + third).astype(bf16)


def halves_kernel(own_ref, other_ref, out_ref):
    half = own_ref.shape[0]
    core = lax.axis_index("core")
    out_ref[pl.ds(pl.multiple_of(core * half, half), half), :] = own_ref[...]
    out_ref[pl.ds(pl.multiple_of((1 - core) * half, half), half), :] = other_ref[...]


def unpack_kernel(feats, got_ref, up_ref, down_ref, sems):
    nx = got_ref.shape[0] // 2
    blocks = up_ref.shape[1] // nx // LANES
    copies = []
    for x in range(nx):
        for s, out in enumerate((up_ref, down_ref)):
            for k in range(blocks):
                copies.append(
                    pltpu.make_async_copy(
                        got_ref.at[2 * x + s, pl.ds(k * feats, feats), :],
                        out.at[:, pl.ds((x * blocks + k) * LANES, LANES)],
                        sems.at[len(copies)],
                    )
                )
                copies[-1].start()
    for copy in copies:
        copy.wait()


def unpack(feats, units, got):
    out = jax.ShapeDtypeStruct((feats, units), bf16)
    hbm = pl.BlockSpec(memory_space=pltpu.HBM)
    return pl.pallas_call(
        functools.partial(unpack_kernel, feats),
        out_shape=(out, out),
        in_specs=[pl.BlockSpec(memory_space=pltpu.VMEM)],
        out_specs=(hbm, hbm),
        scratch_shapes=[pltpu.SemaphoreType.DMA((2 * units // LANES,))],
        compiler_params=pltpu.CompilerParams(vmem_limit_bytes=48 * 1024 * 1024),
        name="unpack",
    )(got)


def exchange(value, axes):
    return lax.all_to_all(value, axes, 0, 0, tiled=True)


def shards(sizes, tokens, grad_out, up_codes, up_scales, down_codes, down_scales):
    nx, nyh, nyl, nzl, ncore = (sizes[a] for a in ("x", "yh", "yl", "zl", "core"))
    feats, units = up_codes.shape
    tok = tokens.shape[0]
    mine = units // nx
    srcs = nx * nyl
    share = tok // (nyh * nyl)
    rows = feats * (mine // LANES)
    S = jax.ShapeDtypeStruct

    packed = pack(nx, tokens, grad_out, up_codes, up_scales, down_codes, down_scales)
    got = exchange(packed, ("x", "yl"))
    part = call(functools.partial(forward_kernel, feats), S((tok, mine), bf16), got, name="forward")
    terms = exchange(part.reshape(nyh * nyl, share, mine), ("yh", "yl"))
    keep, send = call(
        sum_kernel, (S((2, share, mine), f32), S((2, share, mine), bf16)), terms, name="sum"
    )
    other = lax.ppermute(send, "zh", [(0, 1), (1, 0)])
    acts = call(gelu_kernel, S((nyh * nyl, share, mine), bf16), keep, other, name="gelu")
    act = exchange(acts, ("yh", "yl")).reshape(tok, mine)
    half = tok // 2
    swap = [(i, i ^ 1) for i in range(ncore)]
    send = call(
        functools.partial(terms_kernel, feats, True), S((srcs, half, feats), bf16), got, act, name="terms_send"
    )
    other = lax.ppermute(send, "core", swap)
    grads = call(functools.partial(grads_kernel, feats), S((srcs, rows, LANES), bf16), got, act, name="grads")
    keep = call(
        functools.partial(terms_kernel, feats, False), S((srcs, half, feats), f32), got, act, name="terms_keep"
    )
    terms = exchange(call(pair_kernel, S((srcs, half, feats), bf16), keep, other, name="pair"), ("x", "yl"))
    term = call(home_kernel, S((half, feats), f32), terms, name="home")
    other = lax.ppermute(term, "zl", [(i, i ^ 1) for i in range(nzl)])
    term = call(pair_kernel, S((half, feats), bf16), term, other, name="pairs")
    term, grads = lax.optimization_barrier((term, grads))
    home = exchange(grads, ("x", "yl"))
    prev = lax.ppermute(term, "zl", [(i, (i + 2) % nzl) for i in range(nzl)])
    nxt = lax.ppermute(term, "zl", [(i, (i - 2) % nzl) for i in range(nzl)])
    final = call(triple_kernel, S((half, feats), bf16), term, prev, nxt, name="triples")
    grad_tokens = call(
        halves_kernel, S((tok, feats), bf16), final, lax.ppermute(final, "core", swap), name="halves"
    )
    grad_up, grad_down = unpack(feats, units, home)
    return grad_up, grad_down, grad_tokens


AXES = ("x", "yh", "yl", "zh", "zl", "core")
SIZES = (4, 4, 2, 2, 6, 2)


def solution(mesh, sizes=SIZES):
    fine = Mesh(mesh.devices.reshape(sizes), AXES)
    intra, inter = AXES[:4], AXES[4:]
    in_specs = (
        P(None, intra),
        P(None, intra),
        P(intra, inter),
        P(intra, inter),
        P(intra, inter),
        P(intra, inter),
    )
    out_specs = (P(intra, inter), P(intra, inter), P(None, intra))
    return jax.shard_map(
        functools.partial(shards, dict(zip(AXES, sizes))),
        mesh=fine,
        in_specs=in_specs,
        out_specs=out_specs,
        check_vma=False,
    )
```

```python
import functools
import math

import jax
import jax.numpy as jnp
from jax import lax
from jax.experimental import pallas as pl
from jax.experimental.pallas import tpu as pltpu
from jax.sharding import Mesh
from jax.sharding import PartitionSpec as P

coef = math.sqrt(2.0 / math.pi)
f32 = jnp.float32
bf16 = jnp.bfloat16
LANES = 128
SCALE_BLOCK = 256


def gelu_parts(pre):
    inner = coef * (pre + 0.044715 * pre * pre * pre)
    tanh_value = jnp.tanh(inner)
    value = 0.5 * pre * (1.0 + tanh_value)
    slope = 0.5 * (1.0 + tanh_value) + 0.5 * pre * (1.0 - tanh_value * tanh_value) * coef * (
        1.0 + 3.0 * 0.044715 * pre * pre
    )
    return (value, slope)


def call(kernel, out_shape, *args, name):
    vmem = pl.BlockSpec(memory_space=pltpu.VMEM)
    return pl.pallas_call(
        kernel,
        out_shape=out_shape,
        in_specs=[vmem] * len(args),
        out_specs=jax.tree.map(lambda _: vmem, out_shape),
        compiler_params=pltpu.CompilerParams(vmem_limit_bytes=48 * 1024 * 1024),
        name=name,
    )(*args)


def pack_kernel(nx, tok_ref, grad_ref, uc_ref, us_ref, dc_ref, ds_ref, out_ref, codes, scales, acts, packed, sems, act_sems, out_sems):
    feats, units = uc_ref.shape
    width = units // nx
    blocks = width // LANES
    sides = ((uc_ref, us_ref, tok_ref), (dc_ref, ds_ref, grad_ref))
    scale_copies = [
        pltpu.make_async_copy(side[1], scales.at[s], sems.at[s, nx]) for s, side in enumerate(sides)
    ]
    for copy in scale_copies:
        copy.start()
    code_copies = {}
    for x in range(nx):
        for s, side in enumerate(sides):
            cols = pl.ds(x * width, width)
            code_copies[s, x] = pltpu.make_async_copy(
                side[0].at[:, cols], codes.at[s, :, cols], sems.at[s, x]
            )
            code_copies[s, x].start()
    act_copies = [pltpu.make_async_copy(side[2], acts.at[s], act_sems.at[s]) for s, side in enumerate(sides)]
    for copy in act_copies:
        copy.start()
    pending = []
    columns = []
    for s in range(2):
        scale_copies[s].wait()
        columns.append(scales[s].T)
    for x in range(nx):
        for s in range(2):
            code_copies[s, x].wait()
            for k in range(blocks):
                at = (x * blocks + k) * LANES
                b = at // SCALE_BLOCK
                w = codes[s, :, at : at + LANES].astype(f32) * columns[s][:, b : b + 1]
                packed[2 * x + s, k * feats : (k + 1) * feats, :] = w.astype(bf16)
            pending.append(
                pltpu.make_async_copy(
                    packed.at[2 * x + s],
                    out_ref.at[2 * x + s, pl.ds(0, blocks * feats), :],
                    out_sems.at[0, 2 * x + s],
                )
            )
            pending[-1].start()
    for s in range(2):
        act_copies[s].wait()
        for x in range(nx):
            pending.append(
                pltpu.make_async_copy(
                    acts.at[s],
                    out_ref.at[2 * x + s, pl.ds(blocks * feats, tok_ref.shape[0]), :],
                    out_sems.at[1, 2 * x + s],
                )
            )
            pending[-1].start()
    for copy in pending:
        copy.wait()


def pack(nx, tokens, grad_out, up_codes, up_scales, down_codes, down_scales):
    feats, units = up_codes.shape
    tok = tokens.shape[0]
    rows = feats * (units // nx // LANES)
    return pl.pallas_call(
        functools.partial(pack_kernel, nx),
        out_shape=jax.ShapeDtypeStruct((2 * nx, rows + tok, LANES), bf16),
        in_specs=[pl.BlockSpec(memory_space=pltpu.HBM)] * 6,
        out_specs=pl.BlockSpec(memory_space=pltpu.HBM),
        scratch_shapes=[
            pltpu.VMEM((2, feats, units), jnp.int32),
            pltpu.VMEM((2, units // SCALE_BLOCK, feats), f32),
            pltpu.VMEM((2, tok, LANES), bf16),
            pltpu.VMEM((2 * nx, rows, LANES), bf16),
            pltpu.SemaphoreType.DMA((2, nx + 1)),
            pltpu.SemaphoreType.DMA((2,)),
            pltpu.SemaphoreType.DMA((2, 2 * nx)),
        ],
        compiler_params=pltpu.CompilerParams(vmem_limit_bytes=56 * 1024 * 1024),
        name="pack",
    )(tokens, grad_out, up_codes, up_scales.T, down_codes, down_scales.T)


def weights(ref, feats, sources, blocks):
    return jnp.concatenate(
        [
            jnp.concatenate([ref[s, k * feats : (k + 1) * feats, :] for k in blocks], axis=1)
            for s in sources
        ],
        axis=0,
    )


def forward_kernel(feats, got_ref, out_ref):
    srcs = got_ref.shape[0]
    blocks = out_ref.shape[1] // LANES
    for k in range(0, blocks, 2):
        ks = range(k, min(k + 2, blocks))
        total = None
        for s in range(0, srcs, 2):
            acts = jnp.concatenate([got_ref[s + i, blocks * feats :, :] for i in range(2)], axis=1)
            part = jnp.dot(acts, weights(got_ref, feats, (s, s + 1), ks), preferred_element_type=f32)
            total = part if total is None else total + part
        out_ref[:, k * LANES : (k + len(ks)) * LANES] = total.astype(bf16)


def sum_kernel(got_ref, keep_ref, send_ref):
    for s in range(2):
        total = got_ref[s].astype(f32)
        for h in range(1, got_ref.shape[0] // 2):
            total = total + got_ref[2 * h + s].astype(f32)
        keep_ref[s] = total
        send_ref[s] = total.astype(bf16)


def gelu_kernel(keep_ref, got_ref, out_ref):
    pre = keep_ref[0] + got_ref[0].astype(f32)
    back = keep_ref[1] + got_ref[1].astype(f32)
    value, slope = gelu_parts(pre)
    hidden = value.astype(bf16)
    dpre = (back * slope).astype(bf16)
    for h in range(out_ref.shape[0] // 2):
        out_ref[2 * h] = dpre
        out_ref[2 * h + 1] = hidden


def terms_kernel(feats, theirs, got_ref, act_ref, out_ref):
    blocks = act_ref.shape[1] // LANES
    half = act_ref.shape[0] // 2
    core = lax.axis_index("core")
    start = pl.multiple_of((1 - core if theirs else core) * half, half)
    act = act_ref[pl.ds(start, half), :]
    for s in range(0, got_ref.shape[0], 2):
        total = None
        for k in range(0, blocks, 2):
            ks = range(k, min(k + 2, blocks))
            part = lax.dot_general(
                act[:, k * LANES : (k + len(ks)) * LANES],
                weights(got_ref, feats, (s, s + 1), ks),
                (((1,), (1,)), ((), ())),
                preferred_element_type=f32,
            )
            total = part if total is None else total + part
        for i in range(2):
            out_ref[s + i] = total[:, i * feats : (i + 1) * feats].astype(out_ref.dtype)


def grads_kernel(feats, got_ref, act_ref, out_ref):
    blocks = act_ref.shape[1] // LANES
    act = act_ref[...]
    for s in range(got_ref.shape[0]):
        acts = got_ref[s, blocks * feats :, :]
        grad = lax.dot_general(acts, act, (((0,), (0,)), ((), ())), preferred_element_type=f32)
        for k in range(blocks):
            out_ref[s, k * feats : (k + 1) * feats, :] = grad[:, k * LANES : (k + 1) * LANES].astype(bf16)


def pair_kernel(keep_ref, got_ref, out_ref):
    out_ref[...] = (keep_ref[...] + got_ref[...].astype(f32)).astype(bf16)


def home_kernel(got_ref, out_ref):
    total = got_ref[0].astype(f32)
    for x in range(1, got_ref.shape[0] // 2):
        total = total + got_ref[2 * x].astype(f32)
    out_ref[...] = total


def triple_kernel(own_ref, prev_ref, next_ref, out_ref):
    pos = lax.div(lax.axis_index("zl"), 2)
    own, prev, nxt = (r[...].astype(f32) for r in (own_ref, prev_ref, next_ref))
    first = jnp.where(pos == 0, own, jnp.where(pos == 1, prev, nxt))
    second = jnp.where(pos == 1, own, jnp.where(pos == 2, prev, nxt))
    third = jnp.where(pos == 2, own, jnp.where(pos == 0, prev, nxt))
    out_ref[...] = (first + second + third).astype(bf16)


def halves_kernel(own_ref, other_ref, out_ref):
    half = own_ref.shape[0]
    core = lax.axis_index("core")
    out_ref[pl.ds(pl.multiple_of(core * half, half), half), :] = own_ref[...]
    out_ref[pl.ds(pl.multiple_of((1 - core) * half, half), half), :] = other_ref[...]


def unpack_kernel(feats, got_ref, up_ref, down_ref, sems):
    nx = got_ref.shape[0] // 2
    blocks = up_ref.shape[1] // nx // LANES
    copies = []
    for x in range(nx):
        for s, out in enumerate((up_ref, down_ref)):
            for k in range(blocks):
                copies.append(
                    pltpu.make_async_copy(
                        got_ref.at[2 * x + s, pl.ds(k * feats, feats), :],
                        out.at[:, pl.ds((x * blocks + k) * LANES, LANES)],
                        sems.at[len(copies)],
                    )
                )
                copies[-1].start()
    for copy in copies:
        copy.wait()


def unpack(feats, units, got):
    out = jax.ShapeDtypeStruct((feats, units), bf16)
    hbm = pl.BlockSpec(memory_space=pltpu.HBM)
    return pl.pallas_call(
        functools.partial(unpack_kernel, feats),
        out_shape=(out, out),
        in_specs=[pl.BlockSpec(memory_space=pltpu.VMEM)],
        out_specs=(hbm, hbm),
        scratch_shapes=[pltpu.SemaphoreType.DMA((2 * units // LANES,))],
        compiler_params=pltpu.CompilerParams(vmem_limit_bytes=48 * 1024 * 1024),
        name="unpack",
    )(got)


def exchange(value, axes):
    return lax.all_to_all(value, axes, 0, 0, tiled=True)


def shards(sizes, tokens, grad_out, up_codes, up_scales, down_codes, down_scales):
    nx, nyh, nyl, nzl, ncore = (sizes[a] for a in ("x", "yh", "yl", "zl", "core"))
    feats, units = up_codes.shape
    tok = tokens.shape[0]
    mine = units // nx
    srcs = nx * nyl
    share = tok // (nyh * nyl)
    rows = feats * (mine // LANES)
    S = jax.ShapeDtypeStruct

    packed = pack(nx, tokens, grad_out, up_codes, up_scales, down_codes, down_scales)
    got = exchange(packed, ("x", "yl"))
    part = call(functools.partial(forward_kernel, feats), S((tok, mine), bf16), got, name="forward")
    terms = exchange(part.reshape(nyh * nyl, share, mine), ("yh", "yl"))
    keep, send = call(
        sum_kernel, (S((2, share, mine), f32), S((2, share, mine), bf16)), terms, name="sum"
    )
    other = lax.ppermute(send, "zh", [(0, 1), (1, 0)])
    acts = call(gelu_kernel, S((nyh * nyl, share, mine), bf16), keep, other, name="gelu")
    act = exchange(acts, ("yh", "yl")).reshape(tok, mine)
    half = tok // 2
    swap = [(i, i ^ 1) for i in range(ncore)]
    send = call(
        functools.partial(terms_kernel, feats, True), S((srcs, half, feats), bf16), got, act, name="terms_send"
    )
    other = lax.ppermute(send, "core", swap)
    grads = call(functools.partial(grads_kernel, feats), S((srcs, rows, LANES), bf16), got, act, name="grads")
    keep = call(
        functools.partial(terms_kernel, feats, False), S((srcs, half, feats), f32), got, act, name="terms_keep"
    )
    terms = exchange(call(pair_kernel, S((srcs, half, feats), bf16), keep, other, name="pair"), ("x", "yl"))
    term = call(home_kernel, S((half, feats), f32), terms, name="home")
    other = lax.ppermute(term, "zl", [(i, i ^ 1) for i in range(nzl)])
    term = call(pair_kernel, S((half, feats), bf16), term, other, name="pairs")
    term, grads = lax.optimization_barrier((term, grads))
    home = exchange(grads, ("x", "yl"))
    prev = lax.ppermute(term, "zl", [(i, (i + 2) % nzl) for i in range(nzl)])
    nxt = lax.ppermute(term, "zl", [(i, (i - 2) % nzl) for i in range(nzl)])
    final = call(triple_kernel, S((half, feats), bf16), term, prev, nxt, name="triples")
    grad_tokens = call(
        halves_kernel, S((tok, feats), bf16), final, lax.ppermute(final, "core", swap), name="halves"
    )
    grad_up, grad_down = unpack(feats, units, home)
    return grad_up, grad_down, grad_tokens


AXES = ("x", "yh", "yl", "zh", "zl", "core")
SIZES = (4, 4, 2, 2, 6, 2)


def solution(mesh, sizes=SIZES):
    fine = Mesh(mesh.devices.reshape(sizes), AXES)
    intra, inter = AXES[:4], AXES[4:]
    in_specs = (
        P(None, intra),
        P(None, intra),
        P(intra, inter),
        P(intra, inter),
        P(intra, inter),
        P(intra, inter),
    )
    out_specs = (P(intra, inter), P(intra, inter), P(None, intra))
    return jax.shard_map(
        functools.partial(shards, dict(zip(AXES, sizes))),
        mesh=fine,
        in_specs=in_specs,
        out_specs=out_specs,
        check_vma=False,
    )
```

```python
import functools
import math

import jax
import jax.numpy as jnp
from jax import lax
from jax.experimental import pallas as pl
from jax.experimental.pallas import tpu as pltpu
from jax.sharding import Mesh
from jax.sharding import PartitionSpec as P

coef = math.sqrt(2.0 / math.pi)
f32 = jnp.float32
bf16 = jnp.bfloat16
LANES = 128
SCALE_BLOCK = 256


def gelu_parts(pre):
    inner = coef * (pre + 0.044715 * pre * pre * pre)
    tanh_value = jnp.tanh(inner)
    value = 0.5 * pre * (1.0 + tanh_value)
    slope = 0.5 * (1.0 + tanh_value) + 0.5 * pre * (1.0 - tanh_value * tanh_value) * coef * (
        1.0 + 3.0 * 0.044715 * pre * pre
    )
    return (value, slope)


def call(kernel, out_shape, *args, name):
    vmem = pl.BlockSpec(memory_space=pltpu.VMEM)
    return pl.pallas_call(
        kernel,
        out_shape=out_shape,
        in_specs=[vmem] * len(args),
        out_specs=jax.tree.map(lambda _: vmem, out_shape),
        compiler_params=pltpu.CompilerParams(vmem_limit_bytes=48 * 1024 * 1024),
        name=name,
    )(*args)


def pack_kernel(nx, tok_ref, grad_ref, uc_ref, us_ref, dc_ref, ds_ref, out_ref, codes, scales, acts, packed, sems, act_sems, out_sems):
    feats, units = uc_ref.shape
    width = units // nx
    blocks = width // LANES
    sides = ((uc_ref, us_ref, tok_ref), (dc_ref, ds_ref, grad_ref))
    scale_copies = [
        pltpu.make_async_copy(side[1], scales.at[s], sems.at[s, nx]) for s, side in enumerate(sides)
    ]
    for copy in scale_copies:
        copy.start()
    code_copies = {}
    for x in range(nx):
        for s, side in enumerate(sides):
            cols = pl.ds(x * width, width)
            code_copies[s, x] = pltpu.make_async_copy(
                side[0].at[:, cols], codes.at[s, :, cols], sems.at[s, x]
            )
            code_copies[s, x].start()
    act_copies = [pltpu.make_async_copy(side[2], acts.at[s], act_sems.at[s]) for s, side in enumerate(sides)]
    for copy in act_copies:
        copy.start()
    pending = []
    columns = []
    for s in range(2):
        scale_copies[s].wait()
        columns.append(scales[s].T)
    for x in range(nx):
        for s in range(2):
            code_copies[s, x].wait()
            for k in range(blocks):
                at = (x * blocks + k) * LANES
                b = at // SCALE_BLOCK
                w = codes[s, :, at : at + LANES].astype(f32) * columns[s][:, b : b + 1]
                packed[2 * x + s, k * feats : (k + 1) * feats, :] = w.astype(bf16)
            pending.append(
                pltpu.make_async_copy(
                    packed.at[2 * x + s],
                    out_ref.at[2 * x + s, pl.ds(0, blocks * feats), :],
                    out_sems.at[0, 2 * x + s],
                )
            )
            pending[-1].start()
    for s in range(2):
        act_copies[s].wait()
        for x in range(nx):
            pending.append(
                pltpu.make_async_copy(
                    acts.at[s],
                    out_ref.at[2 * x + s, pl.ds(blocks * feats, tok_ref.shape[0]), :],
                    out_sems.at[1, 2 * x + s],
                )
            )
            pending[-1].start()
    for copy in pending:
        copy.wait()


def pack(nx, tokens, grad_out, up_codes, up_scales, down_codes, down_scales):
    feats, units = up_codes.shape
    tok = tokens.shape[0]
    rows = feats * (units // nx // LANES)
    return pl.pallas_call(
        functools.partial(pack_kernel, nx),
        out_shape=jax.ShapeDtypeStruct((2 * nx, rows + tok, LANES), bf16),
        in_specs=[pl.BlockSpec(memory_space=pltpu.HBM)] * 6,
        out_specs=pl.BlockSpec(memory_space=pltpu.HBM),
        scratch_shapes=[
            pltpu.VMEM((2, feats, units), jnp.int32),
            pltpu.VMEM((2, units // SCALE_BLOCK, feats), f32),
            pltpu.VMEM((2, tok, LANES), bf16),
            pltpu.VMEM((2 * nx, rows, LANES), bf16),
            pltpu.SemaphoreType.DMA((2, nx + 1)),
            pltpu.SemaphoreType.DMA((2,)),
            pltpu.SemaphoreType.DMA((2, 2 * nx)),
        ],
        compiler_params=pltpu.CompilerParams(vmem_limit_bytes=56 * 1024 * 1024),
        name="pack",
    )(tokens, grad_out, up_codes, up_scales.T, down_codes, down_scales.T)


def weights(ref, feats, sources, blocks):
    return jnp.concatenate(
        [
            jnp.concatenate([ref[s, k * feats : (k + 1) * feats, :] for k in blocks], axis=1)
            for s in sources
        ],
        axis=0,
    )


def forward_kernel(feats, got_ref, out_ref):
    srcs = got_ref.shape[0]
    blocks = out_ref.shape[1] // LANES
    for k in range(0, blocks, 2):
        ks = range(k, min(k + 2, blocks))
        total = None
        for s in range(0, srcs, 2):
            acts = jnp.concatenate([got_ref[s + i, blocks * feats :, :] for i in range(2)], axis=1)
            part = jnp.dot(acts, weights(got_ref, feats, (s, s + 1), ks), preferred_element_type=f32)
            total = part if total is None else total + part
        out_ref[:, k * LANES : (k + len(ks)) * LANES] = total.astype(bf16)


def sum_kernel(got_ref, keep_ref, send_ref):
    for s in range(2):
        total = got_ref[s].astype(f32)
        for h in range(1, got_ref.shape[0] // 2):
            total = total + got_ref[2 * h + s].astype(f32)
        keep_ref[s] = total
        send_ref[s] = total.astype(bf16)


def gelu_kernel(keep_ref, got_ref, out_ref):
    pre = keep_ref[0] + got_ref[0].astype(f32)
    back = keep_ref[1] + got_ref[1].astype(f32)
    value, slope = gelu_parts(pre)
    hidden = value.astype(bf16)
    dpre = (back * slope).astype(bf16)
    for h in range(out_ref.shape[0] // 2):
        out_ref[2 * h] = dpre
        out_ref[2 * h + 1] = hidden


def terms_kernel(feats, theirs, got_ref, act_ref, out_ref):
    blocks = act_ref.shape[1] // LANES
    half = act_ref.shape[0] // 2
    core = lax.axis_index("core")
    start = pl.multiple_of((1 - core if theirs else core) * half, half)
    act = act_ref[pl.ds(start, half), :]
    for s in range(0, got_ref.shape[0], 2):
        total = None
        for k in range(0, blocks, 2):
            ks = range(k, min(k + 2, blocks))
            part = lax.dot_general(
                act[:, k * LANES : (k + len(ks)) * LANES],
                weights(got_ref, feats, (s, s + 1), ks),
                (((1,), (1,)), ((), ())),
                preferred_element_type=f32,
            )
            total = part if total is None else total + part
        for i in range(2):
            out_ref[s + i] = total[:, i * feats : (i + 1) * feats].astype(out_ref.dtype)


def grads_kernel(feats, got_ref, act_ref, out_ref):
    blocks = act_ref.shape[1] // LANES
    act = act_ref[...]
    for s in range(got_ref.shape[0]):
        acts = got_ref[s, blocks * feats :, :]
        grad = lax.dot_general(acts, act, (((0,), (0,)), ((), ())), preferred_element_type=f32)
        for k in range(blocks):
            out_ref[s, k * feats : (k + 1) * feats, :] = grad[:, k * LANES : (k + 1) * LANES].astype(bf16)


def pair_kernel(keep_ref, got_ref, out_ref):
    out_ref[...] = (keep_ref[...] + got_ref[...].astype(f32)).astype(bf16)


def home_kernel(got_ref, out_ref):
    total = got_ref[0].astype(f32)
    for x in range(1, got_ref.shape[0] // 2):
        total = total + got_ref[2 * x].astype(f32)
    out_ref[...] = total


def triple_kernel(own_ref, prev_ref, next_ref, out_ref):
    pos = lax.div(lax.axis_index("zl"), 2)
    own, prev, nxt = (r[...].astype(f32) for r in (own_ref, prev_ref, next_ref))
    first = jnp.where(pos == 0, own, jnp.where(pos == 1, prev, nxt))
    second = jnp.where(pos == 1, own, jnp.where(pos == 2, prev, nxt))
    third = jnp.where(pos == 2, own, jnp.where(pos == 0, prev, nxt))
    out_ref[...] = (first + second + third).astype(bf16)


def halves_kernel(own_ref, other_ref, out_ref):
    half = own_ref.shape[0]
    core = lax.axis_index("core")
    out_ref[pl.ds(pl.multiple_of(core * half, half), half), :] = own_ref[...]
    out_ref[pl.ds(pl.multiple_of((1 - core) * half, half), half), :] = other_ref[...]


def unpack_kernel(feats, got_ref, up_ref, down_ref, sems):
    nx = got_ref.shape[0] // 2
    blocks = up_ref.shape[1] // nx // LANES
    copies = []
    for x in range(nx):
        for s, out in enumerate((up_ref, down_ref)):
            for k in range(blocks):
                copies.append(
                    pltpu.make_async_copy(
                        got_ref.at[2 * x + s, pl.ds(k * feats, feats), :],
                        out.at[:, pl.ds((x * blocks + k) * LANES, LANES)],
                        sems.at[len(copies)],
                    )
                )
                copies[-1].start()
    for copy in copies:
        copy.wait()


def unpack(feats, units, got):
    out = jax.ShapeDtypeStruct((feats, units), bf16)
    hbm = pl.BlockSpec(memory_space=pltpu.HBM)
    return pl.pallas_call(
        functools.partial(unpack_kernel, feats),
        out_shape=(out, out),
        in_specs=[pl.BlockSpec(memory_space=pltpu.VMEM)],
        out_specs=(hbm, hbm),
        scratch_shapes=[pltpu.SemaphoreType.DMA((2 * units // LANES,))],
        compiler_params=pltpu.CompilerParams(vmem_limit_bytes=48 * 1024 * 1024),
        name="unpack",
    )(got)


def exchange(value, axes):
    return lax.all_to_all(value, axes, 0, 0, tiled=True)


def shards(sizes, tokens, grad_out, up_codes, up_scales, down_codes, down_scales):
    nx, nyh, nyl, nzl, ncore = (sizes[a] for a in ("x", "yh", "yl", "zl", "core"))
    feats, units = up_codes.shape
    tok = tokens.shape[0]
    mine = units // nx
    srcs = nx * nyl
    share = tok // (nyh * nyl)
    rows = feats * (mine // LANES)
    S = jax.ShapeDtypeStruct

    packed = pack(nx, tokens, grad_out, up_codes, up_scales, down_codes, down_scales)
    got = exchange(packed, ("x", "yl"))
    part = call(functools.partial(forward_kernel, feats), S((tok, mine), bf16), got, name="forward")
    terms = exchange(part.reshape(nyh * nyl, share, mine), ("yh", "yl"))
    keep, send = call(
        sum_kernel, (S((2, share, mine), f32), S((2, share, mine), bf16)), terms, name="sum"
    )
    other = lax.ppermute(send, "zh", [(0, 1), (1, 0)])
    acts = call(gelu_kernel, S((nyh * nyl, share, mine), bf16), keep, other, name="gelu")
    act = exchange(acts, ("yh", "yl")).reshape(tok, mine)
    half = tok // 2
    swap = [(i, i ^ 1) for i in range(ncore)]
    send = call(
        functools.partial(terms_kernel, feats, True), S((srcs, half, feats), bf16), got, act, name="terms_send"
    )
    other = lax.ppermute(send, "core", swap)
    grads = call(functools.partial(grads_kernel, feats), S((srcs, rows, LANES), bf16), got, act, name="grads")
    keep = call(
        functools.partial(terms_kernel, feats, False), S((srcs, half, feats), f32), got, act, name="terms_keep"
    )
    other, grads = lax.optimization_barrier((other, grads))
    terms = exchange(call(pair_kernel, S((srcs, half, feats), bf16), keep, other, name="pair"), ("x", "yl"))
    term = call(home_kernel, S((half, feats), f32), terms, name="home")
    term, grads = lax.optimization_barrier((term, grads))
    grad_up, grad_down = unpack(feats, units, exchange(grads, ("x", "yl")))
    other = lax.ppermute(term, "zl", [(i, i ^ 1) for i in range(nzl)])
    term = call(pair_kernel, S((half, feats), bf16), term, other, name="pairs")
    prev = lax.ppermute(term, "zl", [(i, (i + 2) % nzl) for i in range(nzl)])
    nxt = lax.ppermute(term, "zl", [(i, (i - 2) % nzl) for i in range(nzl)])
    final = call(triple_kernel, S((half, feats), bf16), term, prev, nxt, name="triples")
    other = lax.ppermute(final, "core", swap)
    other, grad_up, grad_down = lax.optimization_barrier((other, grad_up, grad_down))
    grad_tokens = call(halves_kernel, S((tok, feats), bf16), final, other, name="halves")
    return grad_up, grad_down, grad_tokens


AXES = ("x", "yh", "yl", "zh", "zl", "core")
SIZES = (4, 4, 2, 2, 6, 2)


def solution(mesh, sizes=SIZES):
    fine = Mesh(mesh.devices.reshape(sizes), AXES)
    intra, inter = AXES[:4], AXES[4:]
    in_specs = (
        P(None, intra),
        P(None, intra),
        P(intra, inter),
        P(intra, inter),
        P(intra, inter),
        P(intra, inter),
    )
    out_specs = (P(intra, inter), P(intra, inter), P(None, intra))
    return jax.shard_map(
        functools.partial(shards, dict(zip(AXES, sizes))),
        mesh=fine,
        in_specs=in_specs,
        out_specs=out_specs,
        check_vma=False,
    )
```

```python
import functools
import math

import jax
import jax.numpy as jnp
from jax import lax
from jax.experimental import pallas as pl
from jax.experimental.pallas import tpu as pltpu
from jax.sharding import Mesh
from jax.sharding import PartitionSpec as P

coef = math.sqrt(2.0 / math.pi)
f32 = jnp.float32
bf16 = jnp.bfloat16
LANES = 128
SCALE_BLOCK = 256


def gelu_parts(pre):
    inner = coef * (pre + 0.044715 * pre * pre * pre)
    tanh_value = jnp.tanh(inner)
    value = 0.5 * pre * (1.0 + tanh_value)
    slope = 0.5 * (1.0 + tanh_value) + 0.5 * pre * (1.0 - tanh_value * tanh_value) * coef * (
        1.0 + 3.0 * 0.044715 * pre * pre
    )
    return (value, slope)


def call(kernel, out_shape, *args, name):
    vmem = pl.BlockSpec(memory_space=pltpu.VMEM)
    return pl.pallas_call(
        kernel,
        out_shape=out_shape,
        in_specs=[vmem] * len(args),
        out_specs=jax.tree.map(lambda _: vmem, out_shape),
        compiler_params=pltpu.CompilerParams(vmem_limit_bytes=48 * 1024 * 1024),
        name=name,
    )(*args)


def pack_kernel(nx, tok_ref, grad_ref, uc_ref, us_ref, dc_ref, ds_ref, out_ref, codes, scales, acts, packed, sems, act_sems, out_sems):
    feats, units = uc_ref.shape
    width = units // nx
    blocks = width // LANES
    sides = ((uc_ref, us_ref, tok_ref), (dc_ref, ds_ref, grad_ref))
    scale_copies = [
        pltpu.make_async_copy(side[1], scales.at[s], sems.at[s, nx]) for s, side in enumerate(sides)
    ]
    for copy in scale_copies:
        copy.start()
    code_copies = {}
    for x in range(nx):
        for s, side in enumerate(sides):
            cols = pl.ds(x * width, width)
            code_copies[s, x] = pltpu.make_async_copy(
                side[0].at[:, cols], codes.at[s, :, cols], sems.at[s, x]
            )
            code_copies[s, x].start()
    act_copies = [pltpu.make_async_copy(side[2], acts.at[s], act_sems.at[s]) for s, side in enumerate(sides)]
    for copy in act_copies:
        copy.start()
    pending = []
    columns = []
    for s in range(2):
        scale_copies[s].wait()
        columns.append(scales[s].T)
    for x in range(nx):
        for s in range(2):
            code_copies[s, x].wait()
            for k in range(blocks):
                at = (x * blocks + k) * LANES
                b = at // SCALE_BLOCK
                w = codes[s, :, at : at + LANES].astype(f32) * columns[s][:, b : b + 1]
                packed[2 * x + s, k * feats : (k + 1) * feats, :] = w.astype(bf16)
            pending.append(
                pltpu.make_async_copy(
                    packed.at[2 * x + s],
                    out_ref.at[2 * x + s, pl.ds(0, blocks * feats), :],
                    out_sems.at[0, 2 * x + s],
                )
            )
            pending[-1].start()
    for s in range(2):
        act_copies[s].wait()
        for x in range(nx):
            pending.append(
                pltpu.make_async_copy(
                    acts.at[s],
                    out_ref.at[2 * x + s, pl.ds(blocks * feats, tok_ref.shape[0]), :],
                    out_sems.at[1, 2 * x + s],
                )
            )
            pending[-1].start()
    for copy in pending:
        copy.wait()


def pack(nx, tokens, grad_out, up_codes, up_scales, down_codes, down_scales):
    feats, units = up_codes.shape
    tok = tokens.shape[0]
    rows = feats * (units // nx // LANES)
    return pl.pallas_call(
        functools.partial(pack_kernel, nx),
        out_shape=jax.ShapeDtypeStruct((2 * nx, rows + tok, LANES), bf16),
        in_specs=[pl.BlockSpec(memory_space=pltpu.HBM)] * 6,
        out_specs=pl.BlockSpec(memory_space=pltpu.HBM),
        scratch_shapes=[
            pltpu.VMEM((2, feats, units), jnp.int32),
            pltpu.VMEM((2, units // SCALE_BLOCK, feats), f32),
            pltpu.VMEM((2, tok, LANES), bf16),
            pltpu.VMEM((2 * nx, rows, LANES), bf16),
            pltpu.SemaphoreType.DMA((2, nx + 1)),
            pltpu.SemaphoreType.DMA((2,)),
            pltpu.SemaphoreType.DMA((2, 2 * nx)),
        ],
        compiler_params=pltpu.CompilerParams(vmem_limit_bytes=56 * 1024 * 1024),
        name="pack",
    )(tokens, grad_out, up_codes, up_scales.T, down_codes, down_scales.T)


def weights(ref, feats, sources, blocks):
    return jnp.concatenate(
        [
            jnp.concatenate([ref[s, k * feats : (k + 1) * feats, :] for k in blocks], axis=1)
            for s in sources
        ],
        axis=0,
    )


def forward_kernel(feats, got_ref, out_ref):
    srcs = got_ref.shape[0]
    blocks = out_ref.shape[1] // LANES
    for k in range(0, blocks, 2):
        ks = range(k, min(k + 2, blocks))
        total = None
        for s in range(0, srcs, 2):
            acts = jnp.concatenate([got_ref[s + i, blocks * feats :, :] for i in range(2)], axis=1)
            part = jnp.dot(acts, weights(got_ref, feats, (s, s + 1), ks), preferred_element_type=f32)
            total = part if total is None else total + part
        out_ref[:, k * LANES : (k + len(ks)) * LANES] = total.astype(bf16)


def sum_kernel(got_ref, keep_ref, send_ref):
    for s in range(2):
        total = got_ref[s].astype(f32)
        for h in range(1, got_ref.shape[0] // 2):
            total = total + got_ref[2 * h + s].astype(f32)
        keep_ref[s] = total
        send_ref[s] = total.astype(bf16)


def gelu_kernel(keep_ref, got_ref, out_ref):
    pre = keep_ref[0] + got_ref[0].astype(f32)
    back = keep_ref[1] + got_ref[1].astype(f32)
    value, slope = gelu_parts(pre)
    hidden = value.astype(bf16)
    dpre = (back * slope).astype(bf16)
    for h in range(out_ref.shape[0] // 2):
        out_ref[2 * h] = dpre
        out_ref[2 * h + 1] = hidden


def terms_kernel(feats, theirs, got_ref, act_ref, out_ref):
    blocks = act_ref.shape[1] // LANES
    half = act_ref.shape[0] // 2
    core = lax.axis_index("core")
    start = pl.multiple_of((1 - core if theirs else core) * half, half)
    act = act_ref[pl.ds(start, half), :]
    for s in range(0, got_ref.shape[0], 2):
        total = None
        for k in range(0, blocks, 2):
            ks = range(k, min(k + 2, blocks))
            part = lax.dot_general(
                act[:, k * LANES : (k + len(ks)) * LANES],
                weights(got_ref, feats, (s, s + 1), ks),
                (((1,), (1,)), ((), ())),
                preferred_element_type=f32,
            )
            total = part if total is None else total + part
        for i in range(2):
            out_ref[s + i] = total[:, i * feats : (i + 1) * feats].astype(out_ref.dtype)


def grads_kernel(feats, got_ref, act_ref, out_ref):
    blocks = act_ref.shape[1] // LANES
    act = act_ref[...]
    for s in range(got_ref.shape[0]):
        acts = got_ref[s, blocks * feats :, :]
        grad = lax.dot_general(acts, act, (((0,), (0,)), ((), ())), preferred_element_type=f32)
        for k in range(blocks):
            out_ref[s, k * feats : (k + 1) * feats, :] = grad[:, k * LANES : (k + 1) * LANES].astype(bf16)


def pair_kernel(keep_ref, got_ref, out_ref):
    out_ref[...] = (keep_ref[...] + got_ref[...].astype(f32)).astype(bf16)


def home_kernel(got_ref, out_ref):
    total = got_ref[0].astype(f32)
    for x in range(1, got_ref.shape[0] // 2):
        total = total + got_ref[2 * x].astype(f32)
    out_ref[...] = total.astype(bf16)


def reduce_kernel(got_ref, out_ref):
    half = got_ref.shape[1]
    for c in range(2):
        total = got_ref[c].astype(f32)
        for z in range(1, got_ref.shape[0] // 2):
            total = total + got_ref[2 * z + c].astype(f32)
        out_ref[c * half : (c + 1) * half, :] = total.astype(bf16)


def unpack_kernel(feats, got_ref, up_ref, down_ref, sems):
    nx = got_ref.shape[0] // 2
    blocks = up_ref.shape[1] // nx // LANES
    copies = []
    for x in range(nx):
        for s, out in enumerate((up_ref, down_ref)):
            for k in range(blocks):
                copies.append(
                    pltpu.make_async_copy(
                        got_ref.at[2 * x + s, pl.ds(k * feats, feats), :],
                        out.at[:, pl.ds((x * blocks + k) * LANES, LANES)],
                        sems.at[len(copies)],
                    )
                )
                copies[-1].start()
    for copy in copies:
        copy.wait()


def unpack(feats, units, got):
    out = jax.ShapeDtypeStruct((feats, units), bf16)
    hbm = pl.BlockSpec(memory_space=pltpu.HBM)
    return pl.pallas_call(
        functools.partial(unpack_kernel, feats),
        out_shape=(out, out),
        in_specs=[pl.BlockSpec(memory_space=pltpu.VMEM)],
        out_specs=(hbm, hbm),
        scratch_shapes=[pltpu.SemaphoreType.DMA((2 * units // LANES,))],
        compiler_params=pltpu.CompilerParams(vmem_limit_bytes=48 * 1024 * 1024),
        name="unpack",
    )(got)


def exchange(value, axes):
    return lax.all_to_all(value, axes, 0, 0, tiled=True)


def shards(sizes, tokens, grad_out, up_codes, up_scales, down_codes, down_scales):
    nx, nyh, nyl, ncore = (sizes[a] for a in ("x", "yh", "yl", "core"))
    feats, units = up_codes.shape
    tok = tokens.shape[0]
    mine = units // nx
    srcs = nx * nyl
    share = tok // (nyh * nyl)
    rows = feats * (mine // LANES)
    S = jax.ShapeDtypeStruct

    packed = pack(nx, tokens, grad_out, up_codes, up_scales, down_codes, down_scales)
    got = exchange(packed, ("x", "yl"))
    part = call(functools.partial(forward_kernel, feats), S((tok, mine), bf16), got, name="forward")
    terms = exchange(part.reshape(nyh * nyl, share, mine), ("yh", "yl"))
    keep, send = call(
        sum_kernel, (S((2, share, mine), f32), S((2, share, mine), bf16)), terms, name="sum"
    )
    other = lax.ppermute(send, "zh", [(0, 1), (1, 0)])
    acts = call(gelu_kernel, S((nyh * nyl, share, mine), bf16), keep, other, name="gelu")
    act = exchange(acts, ("yh", "yl")).reshape(tok, mine)
    half = tok // 2
    swap = [(i, i ^ 1) for i in range(ncore)]
    send = call(
        functools.partial(terms_kernel, feats, True), S((srcs, half, feats), bf16), got, act, name="terms_send"
    )
    other = lax.ppermute(send, "core", swap)
    grads = call(functools.partial(grads_kernel, feats), S((srcs, rows, LANES), bf16), got, act, name="grads")
    keep = call(
        functools.partial(terms_kernel, feats, False), S((srcs, half, feats), f32), got, act, name="terms_keep"
    )
    terms = exchange(call(pair_kernel, S((srcs, half, feats), bf16), keep, other, name="pair"), ("x", "yl"))
    term = call(home_kernel, S((half, feats), bf16), terms, name="home")
    term, grads = lax.optimization_barrier((term, grads))
    home = exchange(grads, ("x", "yl"))
    halves = lax.all_gather(term, ("zl", "core"), axis=0, tiled=False)
    grad_tokens = call(reduce_kernel, S((tok, feats), bf16), halves, name="reduce")
    grad_up, grad_down = unpack(feats, units, home)
    return grad_up, grad_down, grad_tokens


AXES = ("x", "yh", "yl", "zh", "zl", "core")
SIZES = (4, 4, 2, 2, 6, 2)


def solution(mesh, sizes=SIZES):
    fine = Mesh(mesh.devices.reshape(sizes), AXES)
    intra, inter = AXES[:4], AXES[4:]
    in_specs = (
        P(None, intra),
        P(None, intra),
        P(intra, inter),
        P(intra, inter),
        P(intra, inter),
        P(intra, inter),
    )
    out_specs = (P(intra, inter), P(intra, inter), P(None, intra))
    return jax.shard_map(
        functools.partial(shards, dict(zip(AXES, sizes))),
        mesh=fine,
        in_specs=in_specs,
        out_specs=out_specs,
        check_vma=False,
    )
```
